32 devices in a mesh: lat: 4 (over x, core), lon: 8 (over z, y).
Axes of the slice: x: 2, y: 2, z: 4, core: 2. Of those that a mesh axis runs over, the one named last changes fastest.
Arguments:
- queries: bfloat16 [64, 128, 512], P('lat', 'lon'), may hold values from -12 to 12
- keys: bfloat16 [64, 128, 512], P('lat', 'lon'), may hold values from -12 to 12
- values: bfloat16 [64, 128, 512], P('lat', 'lon'), may hold values from -6 to 6
- out_grad: bfloat16 [64, 128, 512], P('lat', 'lon'), may hold values from -16 to 16
- pos_bias: float32 [8, 13, 13], replicated, may hold values from -0.5 to 0.5
Outputs:
- q_grad: bfloat16 [64, 128, 512], P('lat', 'lon')
- k_grad: bfloat16 [64, 128, 512], P('lat', 'lon')
- v_grad: bfloat16 [64, 128, 512], P('lat', 'lon')
The draws below stay inside these ranges and needn't reach their ends.
All inputs are finite; a program needn't handle non-finite values.
Results may differ from the reference program's by a relative error of at most 0.006.
Values may be sent and summed in bfloat16 or wider, within the bound.
No kernel may reach another device: no remote copies, remote signals or barrier semaphores. Data moves between devices by JAX's collectives and lax.ppermute only.
A program may use at most 64 MiB of HBM per device.

```python
import jax
import jax.numpy as jnp
from jax import lax

D = 512
HEADS = 8
WINDOW = 13
HEAD_DIM = 64
RADIUS = 6
NLAT = 64
NLON = 128


def drawn_field(key, salt):
    field_key = jax.random.fold_in(key, salt)
    return jax.random.truncated_normal(field_key, -6.0, 6.0, (NLAT, NLON, D), jnp.float32)


def draw_queries(key, part):
    field = drawn_field(key, 1)
    return field.astype(jnp.bfloat16)


def draw_keys(key, part):
    field = drawn_field(key, 2)
    return field.astype(jnp.bfloat16)


def block_scale(key, extent, shards, least, largest):
    def one(position, parts):
        draws = jax.random.uniform(jax.random.fold_in(jax.random.fold_in(key, 6), position), (parts,), jnp.float32, least / len(shards), largest / len(shards))
        return jnp.repeat(jnp.exp(draws), extent[position] // parts).reshape((-1,) + (1,) * (len(extent) - position - 1))

    factor_of = one(*shards[0])
    for cut in shards[1:]:
        factor_of = factor_of * one(*cut)
    return factor_of


def scatter_about(rng, dims, width, reach, cuts=(), kind=jnp.bfloat16):
    factor_of = block_scale(rng, dims, cuts, -0.22, 0.18) if cuts else 1.0
    values = jax.random.normal(rng, dims, jnp.float32) * width * factor_of
    return jnp.minimum(jnp.maximum(values, -reach), reach).astype(kind)


def setup_inputs(seed: int = 0) -> dict:
    streams_of = jax.random.split(jax.random.key(seed), 6)
    queries = draw_queries(jax.random.fold_in(streams_of[5], 71), 0)
    keys = draw_keys(jax.random.fold_in(streams_of[5], 71), 0)
    values = scatter_about(streams_of[2], (NLAT, NLON, D), 1.0, 6.0, ((0, 4), (1, 8)))
    out_grad = scatter_about(streams_of[3], (NLAT, NLON, D), 4.0, 16.0, ((0, 4), (1, 8)))
    pos_bias = jnp.clip(jax.random.uniform(streams_of[4], (HEADS, WINDOW, WINDOW), jnp.float32, -0.5, 0.5), -0.5, 0.5)
    return dict(queries=queries, keys=keys, values=values, out_grad=out_grad, pos_bias=pos_bias)


def pad_grid(field):
    wrapped = jnp.concatenate([field[:, NLON - RADIUS:], field, field[:, :RADIUS]], axis=1)
    border = jnp.zeros((RADIUS,) + wrapped.shape[1:], wrapped.dtype)
    return jnp.concatenate([border, wrapped, border], axis=0)


def windows(padded, row_index, flipped):
    band_rows = lax.dynamic_slice_in_dim(padded, row_index, WINDOW, 0)
    if flipped:
        band_rows = band_rows[::-1]
        slice_starts = [WINDOW - 1 - offset_index for offset_index in range(WINDOW)]
    else:
        slice_starts = list(range(WINDOW))
    return jnp.stack([band_rows[:, slice_start:slice_start + NLON] for slice_start in slice_starts], axis=1)


def split_heads(block):
    return block.reshape(block.shape[:-1] + (HEADS, HEAD_DIM)).astype(jnp.float32)


def rounded(field):
    return lax.optimization_barrier(field.astype(jnp.bfloat16)).astype(jnp.float32)


def reference(queries, keys, values, out_grad, pos_bias):
    score_scale = HEAD_DIM ** -0.5
    offset_rows = jnp.arange(WINDOW, dtype=jnp.int32) - RADIUS
    key_pad = pad_grid(keys)
    value_pad = pad_grid(values)

    def query_row(row_index):
        query_heads = split_heads(lax.dynamic_index_in_dim(queries, row_index, 0, keepdims=False))
        grad_heads = split_heads(lax.dynamic_index_in_dim(out_grad, row_index, 0, keepdims=False))
        key_win = split_heads(windows(key_pad, row_index, False))
        value_win = split_heads(windows(value_pad, row_index, False))
        scores = jnp.einsum('xhd,abxhd->xhab', query_heads, key_win) * score_scale + pos_bias[None]
        key_rows = row_index + offset_rows
        valid = ((key_rows >= 0) & (key_rows < NLAT))[None, None, :, None]
        scores = jnp.where(valid, scores, -jnp.inf)
        row_top = jnp.max(scores, axis=(2, 3), keepdims=True)
        log_total = row_top + jnp.log(jnp.sum(jnp.exp(scores - row_top), axis=(2, 3), keepdims=True))
        probability = jnp.exp(scores - log_total)
        prob_grad = jnp.einsum('xhd,abxhd->xhab', grad_heads, value_win)
        row_delta = jnp.sum(probability * prob_grad, axis=(2, 3), keepdims=True)
        score_grad = rounded(probability * (prob_grad - row_delta))
        query_grad = score_scale * jnp.einsum('xhab,abxhd->xhd', score_grad, key_win)
        return query_grad.reshape(NLON, D).astype(jnp.bfloat16), log_total[:, :, 0, 0], row_delta[:, :, 0, 0]

    all_rows = jnp.arange(NLAT, dtype=jnp.int32)
    q_grad, log_totals, deltas = lax.map(query_row, all_rows)

    query_pad = pad_grid(queries)
    grad_pad = pad_grid(out_grad)
    total_pad = pad_grid(log_totals)
    delta_pad = pad_grid(deltas)

    def key_row(row_index):
        key_heads = split_heads(lax.dynamic_index_in_dim(keys, row_index, 0, keepdims=False))
        value_heads = split_heads(lax.dynamic_index_in_dim(values, row_index, 0, keepdims=False))
        query_win = split_heads(windows(query_pad, row_index, True))
        grad_win = split_heads(windows(grad_pad, row_index, True))
        total_win = jnp.transpose(windows(total_pad, row_index, True), (2, 3, 0, 1))
        delta_win = jnp.transpose(windows(delta_pad, row_index, True), (2, 3, 0, 1))
        scores = jnp.einsum('abxhd,xhd->xhab', query_win, key_heads) * score_scale + pos_bias[None]
        query_rows = row_index + RADIUS - jnp.arange(WINDOW, dtype=jnp.int32)
        valid = ((query_rows >= 0) & (query_rows < NLAT))[None, None, :, None]
        probability = jnp.where(valid, jnp.exp(scores - total_win), 0.0)
        prob_grad = jnp.einsum('abxhd,xhd->xhab', grad_win, value_heads)
        score_grad = rounded(probability * (prob_grad - delta_win))
        prob_low = rounded(probability)
        key_grad = score_scale * jnp.einsum('xhab,abxhd->xhd', score_grad, query_win)
        value_grad = jnp.einsum('xhab,abxhd->xhd', prob_low, grad_win)
        return key_grad.reshape(NLON, D).astype(jnp.bfloat16), value_grad.reshape(NLON, D).astype(jnp.bfloat16)

    k_grad, v_grad = lax.map(key_row, all_rows)
    return (q_grad, k_grad, v_grad)
```

```python
import functools
import math

import jax
import jax.numpy as jnp
import numpy as np
from jax import lax
from jax.experimental import pallas as pl
from jax.experimental.pallas import tpu as pltpu
from jax.sharding import PartitionSpec as P

WINDOW = 13
RADIUS = 6
BAND = 4
GROUP = 4
MASKED = -1e30

VMEM = pl.BlockSpec(memory_space=pltpu.VMEM)
SMEM = pl.BlockSpec(memory_space=pltpu.SMEM)


def dot(a, b, dims):
    return lax.dot_general(a, b, (dims, ((), ())), preferred_element_type=jnp.float32)


def dot_nn(a, b):
    return dot(a, b, ((1,), (0,)))


def dot_nt(a, b):
    return dot(a, b, ((1,), (1,)))


def dot_tn(a, b):
    return dot(a, b, ((0,), (0,)))


def params(limit_mib=48):
    return pltpu.CompilerParams(vmem_limit_bytes=limit_mib * 1024 * 1024)


def cost(flops, moved):
    return pl.CostEstimate(flops=flops, bytes_accessed=moved, transcendentals=0)


def pick_matrices(rows, cols):
    pick = np.zeros((2, 2, rows * 2 * RADIUS, rows * cols), np.float32)
    for row in range(rows):
        for kv in range(2):
            for col in range(RADIUS):
                strip = (row * 2 + kv) * RADIUS + col
                pick[0, kv, strip, row * cols + col] = 1
                pick[1, kv, strip, row * cols + cols - RADIUS + col] = 1
    return pick


def slot_of(side, col):
    return col if side == 0 else 8 + col


def spread_matrices(rows, cols):
    spread = np.zeros((2, 2, rows * cols, rows * 2 * RADIUS), np.float32)
    for row in range(rows):
        for kv in range(2):
            for col in range(RADIUS):
                strip = (row * 2 + kv) * RADIUS + col
                for side in range(2):
                    spread[side, kv, row * cols + slot_of(side, col), strip] = 1
    return spread


def pack_lon_kernel(pick_ref, k_ref, v_ref, west_ref, east_ref):
    k = k_ref[...]
    v = v_ref[...]
    for edge, out_ref in ((0, west_ref), (1, east_ref)):
        strip = dot_nn(pick_ref[edge, 0], k) + dot_nn(pick_ref[edge, 1], v)
        out_ref[...] = strip.astype(out_ref.dtype)


def pack_lat_kernel(k_ref, v_ref, q_ref, g_ref, north_ref, south_ref, *, deep, near):
    at = 0
    for ref, count in ((k_ref, deep), (v_ref, deep), (q_ref, near), (g_ref, near)):
        north_ref[at : at + count] = ref[:count]
        south_ref[at : at + count] = ref[ref.shape[0] - count :]
        at += count


def bias_kernel(table_ref, own_ref, lon_ref, *, cols):
    lanes = table_ref.shape[2]
    key_slot = lax.broadcasted_iota(jnp.int32, (cols, lanes), 0)
    lane = lax.broadcasted_iota(jnp.int32, (cols, lanes), 1)
    query_col = lane & (cols - 1)
    band_row = (lane // cols) & (BAND - 1)
    east = key_slot + cols
    west = key_slot - 8 - RADIUS
    lon_col = jnp.where(key_slot < RADIUS, east, jnp.where((key_slot >= 8) & (key_slot < 8 + RADIUS), west, -1000))
    for out_ref, key_col in ((own_ref, key_slot), (lon_ref, lon_col)):
        offset = key_col - query_col + RADIUS
        hits = [offset == b for b in range(WINDOW)]
        blocks = []
        for a in range(WINDOW):
            block = jnp.full((cols, lanes), MASKED, jnp.float32)
            for b in range(WINDOW):
                block = jnp.where(hits[b], table_ref[b, a : a + 1, :], block)
            blocks.append(block)
        for row in range(WINDOW + BAND - 1):
            total = jnp.full((cols, lanes), MASKED, jnp.float32)
            for i in range(BAND):
                if 0 <= row - i < WINDOW:
                    total = jnp.where(band_row == i, blocks[row - i], total)
            out_ref[row * cols : (row + 1) * cols, :] = total


def attend_kernel(
    lat_ref,
    q_ref,
    g_ref,
    k_ref,
    v_ref,
    north_ref,
    south_ref,
    east_ref,
    west_ref,
    corner_n_ref,
    corner_s_ref,
    own_bias_ref,
    lon_bias_ref,
    spread_ref,
    pick_lon_ref,
    q_grad_ref,
    k_part_ref,
    v_part_ref,
    to_east_ref,
    to_west_ref,
    k_all,
    v_all,
    q_all,
    g_all,
    k_sum,
    v_sum,
    q_sum,
    *,
    rows,
    cols,
    head_size,
    scale,
):
    tokens = rows * cols
    deep = 2 * RADIUS * cols
    near = RADIUS * cols
    lat = lat_ref[0]
    lat_count = lat_ref[1]
    has_north = lat > 0
    has_south = lat < lat_count - 1
    small = jnp.bfloat16

    for kv, own_ref, all_ref in ((0, k_ref, k_all), (1, v_ref, v_all)):
        all_ref[0, :deep] = north_ref[kv * deep : (kv + 1) * deep]
        all_ref[0, deep : deep + tokens] = own_ref[...]
        all_ref[0, deep + tokens :] = south_ref[kv * deep : (kv + 1) * deep]
        strip = 2 * RADIUS * 2 * RADIUS
        to_slots = [spread_ref[side, kv] for side in range(2)]
        to_deep = [m[:deep, :strip] for m in to_slots]
        all_ref[1, deep : deep + tokens] = (
            dot_nn(to_slots[0], east_ref[...]) + dot_nn(to_slots[1], west_ref[...])
        ).astype(small)
        for corner_ref, at in ((corner_n_ref, 0), (corner_s_ref, deep + tokens)):
            all_ref[1, at : at + deep] = (
                dot_nn(to_deep[0], corner_ref[:strip]) + dot_nn(to_deep[1], corner_ref[strip:])
            ).astype(small)
    for at, own_ref, all_ref, factor in ((2 * deep, q_ref, q_all, scale), (2 * deep + near, g_ref, g_all, 1.0)):
        north = north_ref[at : at + near]
        south = south_ref[at : at + near]
        all_ref[:near] = jnp.where(has_north, north * factor, 0).astype(small)
        all_ref[near : near + tokens] = (own_ref[...] * factor).astype(small)
        all_ref[near + tokens :] = jnp.where(has_south, south * factor, 0).astype(small)
    k_sum[...] = jnp.zeros_like(k_sum)
    v_sum[...] = jnp.zeros_like(v_sum)

    band_tokens = BAND * cols
    reach = (BAND + 2 * RADIUS) * cols
    width = GROUP * head_size
    band_count = (rows + 2 * RADIUS) // BAND
    group_count = q_ref.shape[1] // width
    row_head = lax.broadcasted_iota(jnp.int32, (GROUP * band_tokens, width), 0) // band_tokens
    lane_head = lax.broadcasted_iota(jnp.int32, (GROUP * band_tokens, width), 1) // head_size
    diagonal = row_head == lane_head
    key_row = lax.broadcasted_iota(jnp.int32, (reach, 1), 0) // cols
    out_head = lax.broadcasted_iota(jnp.int32, (band_tokens, width), 1) // head_size

    def stacked(block):
        return jnp.where(diagonal, jnp.concatenate([block] * GROUP, axis=0), 0)

    for group in range(group_count):
        lanes = slice(group * width, (group + 1) * width)

        def band_step(band, carry):
            start = pl.multiple_of(band * band_tokens, band_tokens)
            query = stacked(q_all[pl.ds(start, band_tokens), lanes])
            grad = stacked(g_all[pl.ds(start, band_tokens), lanes])
            row = key_row + (band * BAND + lat * rows - 2 * RADIUS)
            off_grid = jnp.where((row >= 0) & (row < lat_count * rows), 0.0, MASKED)
            scores = []
            grads = []
            for part, bias_ref in ((0, own_bias_ref), (1, lon_bias_ref)):
                key = k_all[part, pl.ds(start, reach), lanes]
                value = v_all[part, pl.ds(start, reach), lanes]
                bias = bias_ref[:, group * GROUP * band_tokens : (group + 1) * GROUP * band_tokens]
                scores.append(dot_nt(key, query) + bias + off_grid)
                grads.append(dot_nt(value, grad))
            top = jnp.maximum(
                jnp.max(scores[0], axis=0, keepdims=True), jnp.max(scores[1], axis=0, keepdims=True)
            )
            weights = [jnp.exp(score - top) for score in scores]
            total = sum(jnp.sum(weight, axis=0, keepdims=True) for weight in weights)
            inverse = 1.0 / total
            delta = (
                sum(
                    jnp.sum(weight * slope, axis=0, keepdims=True)
                    for weight, slope in zip(weights, grads)
                )
                * inverse
            )
            q_part = None
            for part in range(2):
                prob = weights[part] * inverse
                score_grad = (prob * (grads[part] - delta)).astype(small)
                k_sum[part, pl.ds(start, reach), lanes] += dot_nn(score_grad, query)
                v_sum[part, pl.ds(start, reach), lanes] += dot_nn(prob.astype(small), grad)
                key = k_all[part, pl.ds(start, reach), lanes]
                term = dot_tn(score_grad, key)
                q_part = term if q_part is None else q_part + term
            mine = q_part[:band_tokens]
            for head in range(1, GROUP):
                mine = jnp.where(out_head == head, q_part[head * band_tokens : (head + 1) * band_tokens], mine)
            q_sum[pl.ds(start, band_tokens), lanes] = mine
            return carry

        lax.fori_loop(0, band_count, band_step, 0)

    q_grad_ref[...] = (q_sum[near : near + tokens] * scale).astype(small)
    k_part_ref[...] = k_sum[0, deep : deep + tokens]
    v_part_ref[...] = v_sum[0, deep : deep + tokens]
    k_lon = k_sum[1, deep : deep + tokens].astype(small)
    v_lon = v_sum[1, deep : deep + tokens].astype(small)
    for side, out_ref in ((0, to_east_ref), (1, to_west_ref)):
        out_ref[...] = (dot_nn(pick_lon_ref[side, 0], k_lon) + dot_nn(pick_lon_ref[side, 1], v_lon)).astype(small)


def finish_kernel(place_ref, k_part_ref, v_part_ref, from_west_ref, from_east_ref, k_grad_ref, v_grad_ref):
    for kv, part_ref, out_ref in ((0, k_part_ref, k_grad_ref), (1, v_part_ref, v_grad_ref)):
        total = part_ref[...]
        total += dot_nn(place_ref[0, kv], from_west_ref[...])
        total += dot_nn(place_ref[1, kv], from_east_ref[...])
        out_ref[...] = total.astype(out_ref.dtype)


def ring(axis, step):
    count = lax.axis_size(axis)
    return [(i, (i + step) % count) for i in range(count)]


def on_device(queries, keys, values, out_grad, pos_bias):
    rows, cols, model_width = queries.shape
    heads = pos_bias.shape[0]
    head_size = model_width // heads
    scale = head_size**-0.5
    tokens = rows * cols
    deep = 2 * RADIUS * cols
    near = RADIUS * cols
    strip = rows * 2 * RADIUS
    small = jnp.bfloat16
    q, k, v, g = (x.reshape(tokens, model_width) for x in (queries, keys, values, out_grad))

    def shape(count, dtype=small):
        return jax.ShapeDtypeStruct((count, model_width), dtype)

    pick = pick_matrices(rows, cols)
    spread = spread_matrices(rows, cols)
    pick_edge = jnp.asarray(pick, small)
    place_edge = jnp.asarray(pick.transpose(0, 1, 3, 2), small)
    spread_lon = jnp.asarray(spread, small)
    pick_lon = jnp.asarray(spread.transpose(0, 1, 3, 2), small)

    west_edge, east_edge = pl.pallas_call(
        pack_lon_kernel,
        out_shape=(shape(strip), shape(strip)),
        in_specs=[VMEM] * 3,
        out_specs=(VMEM, VMEM),
        compiler_params=params(),
        name="pack_lon",
    )(pick_edge, k, v)
    from_east = lax.ppermute(west_edge, "lon", ring("lon", -1))
    from_west = lax.ppermute(east_edge, "lon", ring("lon", 1))

    north_edge, south_edge = pl.pallas_call(
        functools.partial(pack_lat_kernel, deep=deep, near=near),
        out_shape=(shape(2 * deep + 2 * near), shape(2 * deep + 2 * near)),
        in_specs=[VMEM] * 4,
        out_specs=(VMEM, VMEM),
        compiler_params=params(),
        name="pack_lat",
    )(k, v, q, g)
    from_south = lax.ppermute(north_edge, "lat", ring("lat", -1))
    from_north = lax.ppermute(south_edge, "lat", ring("lat", 1))

    lanes = heads * BAND * cols
    table = jnp.transpose(pos_bias, (2, 1, 0))
    table = jnp.repeat(table, BAND * cols, axis=2)
    bias_shape = jax.ShapeDtypeStruct(((WINDOW + BAND - 1) * cols, lanes), jnp.float32)
    own_bias, lon_bias = pl.pallas_call(
        functools.partial(bias_kernel, cols=cols),
        out_shape=(bias_shape, bias_shape),
        in_specs=[VMEM],
        out_specs=(VMEM, VMEM),
        compiler_params=params(),
        cost_estimate=cost(4_000_000, 2_000_000),
        name="bias",
    )(table)

    part = 2 * RADIUS * 2 * RADIUS
    to_north = jnp.concatenate([from_east[:part], from_west[:part]], axis=0)
    to_south = jnp.concatenate([from_east[strip - part :], from_west[strip - part :]], axis=0)
    corner_south = lax.ppermute(to_north, "lat", ring("lat", -1))
    corner_north = lax.ppermute(to_south, "lat", ring("lat", 1))

    lat_place = jnp.stack([lax.axis_index("lat"), jnp.int32(lax.axis_size("lat"))]).astype(jnp.int32)
    ext = tokens + 2 * deep
    wide = tokens + 2 * near
    q_grad, k_part, v_part, to_east, to_west = pl.pallas_call(
        functools.partial(attend_kernel, rows=rows, cols=cols, head_size=head_size, scale=scale),
        out_shape=(
            shape(tokens),
            shape(tokens, jnp.float32),
            shape(tokens, jnp.float32),
            shape(strip),
            shape(strip),
        ),
        in_specs=[SMEM] + [VMEM] * 14,
        out_specs=(VMEM,) * 5,
        scratch_shapes=[
            pltpu.VMEM((2, ext, model_width), small),
            pltpu.VMEM((2, ext, model_width), small),
            pltpu.VMEM((wide, model_width), small),
            pltpu.VMEM((wide, model_width), small),
            pltpu.VMEM((2, ext, model_width), jnp.float32),
            pltpu.VMEM((2, ext, model_width), jnp.float32),
            pltpu.VMEM((wide, model_width), jnp.float32),
        ],
        compiler_params=params(),
        name="attend",
    )(
        lat_place,
        q,
        g,
        k,
        v,
        from_north,
        from_south,
        from_east,
        from_west,
        corner_north,
        corner_south,
        own_bias,
        lon_bias,
        spread_lon,
        pick_lon,
    )
    back_west = lax.ppermute(to_east, "lon", ring("lon", 1))
    back_east = lax.ppermute(to_west, "lon", ring("lon", -1))
    k_grad, v_grad = pl.pallas_call(
        finish_kernel,
        out_shape=(shape(tokens), shape(tokens)),
        in_specs=[VMEM] * 5,
        out_specs=(VMEM, VMEM),
        compiler_params=params(),
        name="finish",
    )(place_edge, k_part, v_part, back_west, back_east)
    return tuple(x.reshape(queries.shape) for x in (q_grad, k_grad, v_grad))


def solution(mesh):
    placed = P("lat", "lon", None)
    return jax.shard_map(
        on_device,
        mesh=mesh,
        in_specs=(placed, placed, placed, placed, P()),
        out_specs=(placed, placed, placed),
        check_vma=False,
    )
```

```python
import functools

import jax
import jax.numpy as jnp
from jax import lax
from jax.experimental import pallas as pl
from jax.experimental.pallas import tpu as pltpu
from jax.sharding import PartitionSpec as P

WINDOW = 13
RADIUS = 6
BAND = 4
GROUP = 4
WEST_SLOT = 8
MASKED = -1e30

ANY = pl.BlockSpec(memory_space=pl.ANY)
VMEM = pl.BlockSpec(memory_space=pltpu.VMEM)


def dot(a, b, dims):
    return lax.dot_general(a, b, (dims, ((), ())), preferred_element_type=jnp.float32)


def dot_nn(a, b):
    return dot(a, b, ((1,), (0,)))


def dot_nt(a, b):
    return dot(a, b, ((1,), (1,)))


def dot_tn(a, b):
    return dot(a, b, ((0,), (0,)))


def iota(shape, dim):
    return lax.broadcasted_iota(jnp.int32, shape, dim)


def low_bits(x, size):
    return x & (size - 1)


def high_bits(x, size):
    return lax.shift_right_logical(x, jnp.int32(size.bit_length() - 1))


def edge_column(token, cols, edge):
    col = low_bits(token, cols) - (0 if edge == 0 else cols - RADIUS)
    return col, (col >= 0) & (col < RADIUS)


def slot_column(token, cols, side):
    col = low_bits(token, cols) - (0 if side == 0 else WEST_SLOT)
    return col, (col >= 0) & (col < RADIUS)


def strip_pick(rows, cols, column_of, which, pair):
    shape = (rows * 2 * RADIUS, rows * cols)
    token = iota(shape, 1)
    col, inside = column_of(token, cols, which)
    target = jnp.where(inside, high_bits(token, cols) * (2 * RADIUS) + pair * RADIUS + col, -1)
    return jnp.where(iota(shape, 0) == target, 1.0, 0.0).astype(jnp.bfloat16)


def strip_place(rows, cols, column_of, which, pair):
    shape = (rows * cols, rows * 2 * RADIUS)
    token = iota(shape, 0)
    col, inside = column_of(token, cols, which)
    target = jnp.where(inside, high_bits(token, cols) * (2 * RADIUS) + pair * RADIUS + col, -1)
    return jnp.where(iota(shape, 1) == target, 1.0, 0.0).astype(jnp.bfloat16)


def run_copies(copies):
    for copy in copies:
        copy.start()
    for copy in copies:
        copy.wait()


def pack_lon_kernel(k_hbm, v_hbm, west_ref, east_ref, k_ref, v_ref, sems, *, rows, cols):
    copies = [
        pltpu.make_async_copy(k_hbm, k_ref, sems.at[0]),
        pltpu.make_async_copy(v_hbm, v_ref, sems.at[1]),
    ]
    for copy in copies:
        copy.start()
    picks = [[strip_pick(rows, cols, edge_column, edge, kv) for kv in range(2)] for edge in range(2)]
    for copy in copies:
        copy.wait()
    k = k_ref[...]
    v = v_ref[...]
    for edge, out_ref in ((0, west_ref), (1, east_ref)):
        out_ref[...] = (dot_nn(picks[edge][0], k) + dot_nn(picks[edge][1], v)).astype(out_ref.dtype)


def pack_lat_kernel(k_ref, v_ref, q_ref, g_ref, order_ref, a_ref, b_ref, sems, *, deep, near):
    odd = lax.rem(lax.axis_index("lat"), 2)

    def copies(north_ref, south_ref):
        found = []
        at = 0
        for ref, count in ((k_ref, deep), (v_ref, deep), (q_ref, near), (g_ref, near)):
            place = pl.ds(at, count)
            found.append((ref.at[pl.ds(0, count)], north_ref.at[place]))
            found.append((ref.at[pl.ds(ref.shape[0] - count, count)], south_ref.at[place]))
            at += count
        return [pltpu.make_async_copy(src, dst, sems.at[i]) for i, (src, dst) in enumerate(found)]

    @pl.when(odd == 1)
    def _():
        run_copies(copies(a_ref, b_ref))

    @pl.when(odd == 0)
    def _():
        run_copies(copies(b_ref, a_ref))


def pack_corner_kernel(east_ref, west_ref, order_ref, a_ref, b_ref, *, part):
    odd = lax.rem(lax.axis_index("lat"), 2)

    def fill(north_ref, south_ref):
        for at, ref in ((0, east_ref), (part, west_ref)):
            north_ref[at : at + part] = ref[:part]
            south_ref[at : at + part] = ref[ref.shape[0] - part :]

    @pl.when(odd == 1)
    def _():
        fill(a_ref, b_ref)

    @pl.when(odd == 0)
    def _():
        fill(b_ref, a_ref)


def bias_kernel(bias_ref, order_ref, own_ref, lon_ref, *, cols):
    heads = bias_ref.shape[0]
    lanes = own_ref.shape[1]
    per_head = lanes // heads
    expand = jnp.where(iota((heads, lanes), 0) == high_bits(iota((heads, lanes), 1), per_head), 1.0, 0.0)
    table = [
        lax.dot_general(
            bias_ref[:, a, :],
            expand,
            (((0,), (0,)), ((), ())),
            precision=lax.Precision.HIGHEST,
            preferred_element_type=jnp.float32,
        )
        for a in range(WINDOW)
    ]
    key_slot = iota((cols, lanes), 0)
    lane = iota((cols, lanes), 1)
    query_col = low_bits(lane, cols)
    band_row = low_bits(high_bits(lane, cols), BAND)
    east = key_slot + cols
    west = key_slot - WEST_SLOT - RADIUS
    far = -4 * cols
    lon_col = jnp.where(
        key_slot < RADIUS, east, jnp.where((key_slot >= WEST_SLOT) & (key_slot < WEST_SLOT + RADIUS), west, far)
    )
    for out_ref, key_col in ((own_ref, key_slot), (lon_ref, lon_col)):
        offset = key_col - query_col + RADIUS
        hits = [offset == b for b in range(WINDOW)]
        blocks = []
        for a in range(WINDOW):
            block = jnp.full((cols, lanes), MASKED, jnp.float32)
            for b in range(WINDOW):
                block = jnp.where(hits[b], table[a][b : b + 1, :], block)
            blocks.append(block)
        for row in range(WINDOW + BAND - 1):
            total = jnp.full((cols, lanes), MASKED, jnp.float32)
            for i in range(BAND):
                if 0 <= row - i < WINDOW:
                    total = jnp.where(band_row == i, blocks[row - i], total)
            out_ref[row * cols : (row + 1) * cols, :] = total


class Plan:
    def __init__(self, rows, cols, width, head_size):
        self.rows, self.cols, self.head_size = rows, cols, head_size
        self.tokens = rows * cols
        self.deep = 2 * RADIUS * cols
        self.near = RADIUS * cols
        self.ext = self.tokens + 2 * self.deep
        self.wide = self.tokens + 2 * self.near
        self.band = BAND * cols
        self.reach = (BAND + 2 * RADIUS) * cols
        self.lanes = GROUP * head_size
        self.stack = GROUP * self.band
        self.groups = width // self.lanes
        self.bands = self.wide // self.band
        self.strip = rows * 2 * RADIUS
        self.part = 2 * RADIUS * 2 * RADIUS

    def pieces(self, band):
        low, high = band * self.band, band * self.band + self.reach
        first, last = self.deep, self.deep + self.tokens
        cuts = ((low, min(high, first), -1), (max(low, first), min(high, last), 0), (max(low, last), high, 1))
        return [cut for cut in cuts if cut[0] < cut[1]]

    def answers(self, band):
        low = band * self.band
        return low < self.near + self.tokens and low + self.band > self.near

    def group_lanes(self, group):
        return slice(group * self.lanes, (group + 1) * self.lanes)

    def bias_lanes(self, group):
        return slice(group * self.stack, (group + 1) * self.stack)

    def stat_row(self, band, group):
        row = group * 8 + band
        return slice(row, row + 1)

    def stacked(self, block):
        shape = (self.stack, self.lanes)
        diagonal = high_bits(iota(shape, 0), self.band) == high_bits(iota(shape, 1), self.head_size)
        return jnp.where(diagonal, jnp.concatenate([block] * GROUP, axis=0), 0)

    def heads_of(self, product):
        head = high_bits(iota((self.band, self.lanes), 1), self.head_size)
        kept = product[: self.band]
        for h in range(1, GROUP):
            kept = jnp.where(head == h, product[h * self.band : (h + 1) * self.band], kept)
        return kept


def edge_masks():
    lat = lax.axis_index("lat")
    north = jnp.where(lat > 0, 0.0, MASKED)
    south = jnp.where(lat < lax.axis_size("lat") - 1, 0.0, MASKED)
    return {-1: north, 0: None, 1: south}


def score_pieces(plan, band, group, k_ref, v_ref, bias_ref, query, grad, masks, kept=None):
    lanes = plan.group_lanes(group)
    out = []
    for start, stop, place in plan.pieces(band):
        if kept is not None and not kept(place):
            continue
        local = slice(start - band * plan.band, stop - band * plan.band)
        score = dot_nt(k_ref[start:stop, lanes], query) + bias_ref[local, plan.bias_lanes(group)]
        if masks[place] is not None:
            score = score + masks[place]
        slope = dot_nt(v_ref[start:stop, lanes], grad)
        out.append((start, stop, place, score, slope))
    return out


def top_of(pieces):
    top = None
    for _, _, _, score, _ in pieces:
        peak = jnp.max(score, axis=0, keepdims=True)
        top = peak if top is None else jnp.maximum(top, peak)
    return top


def sums_of(pieces, top):
    total = 0.0
    drift = 0.0
    weights = []
    for _, _, _, score, slope in pieces:
        weight = jnp.exp(score - top)
        weights.append(weight)
        total = total + jnp.sum(weight, axis=0, keepdims=True)
        drift = drift + jnp.sum(weight * slope, axis=0, keepdims=True)
    return weights, total, drift


def own_stats_kernel(
    q_ref, g_ref, k_ref, v_ref, a_ref, b_ref, bias_ref, order_ref, q_all, g_all, k_all, v_all, stats_ref, *, plan, scale
):
    deep, near, tokens = plan.deep, plan.near, plan.tokens
    lat = lax.axis_index("lat")
    odd = lax.rem(lat, 2)
    has_north = lat > 0
    has_south = lat < lax.axis_size("lat") - 1

    def halos(north_ref, south_ref):
        for kv, all_ref in ((0, k_all), (1, v_all)):
            all_ref[:deep] = north_ref[kv * deep : (kv + 1) * deep]
            all_ref[deep + tokens :] = south_ref[kv * deep : (kv + 1) * deep]
        for at, all_ref, factor in ((2 * deep, q_all, scale), (2 * deep + near, g_all, None)):
            for there, edge_ref, place in (
                (has_north, north_ref, slice(0, near)),
                (has_south, south_ref, slice(near + tokens, near + tokens + near)),
            ):
                edge = edge_ref[at : at + near]
                edge = edge if factor is None else edge * factor
                all_ref[place] = jnp.where(there, edge, jnp.zeros_like(edge))

    @pl.when(odd == 1)
    def _():
        halos(a_ref, b_ref)

    @pl.when(odd == 0)
    def _():
        halos(b_ref, a_ref)

    k_all[deep : deep + tokens] = k_ref[...]
    v_all[deep : deep + tokens] = v_ref[...]
    q_all[near : near + tokens] = q_ref[...] * scale
    g_all[near : near + tokens] = g_ref[...]
    masks = edge_masks()
    for band in range(plan.bands):
        for group in range(plan.groups):
            lanes = plan.group_lanes(group)
            place = slice(band * plan.band, (band + 1) * plan.band)
            query = plan.stacked(q_all[place, lanes])
            grad = plan.stacked(g_all[place, lanes])
            pieces = score_pieces(plan, band, group, k_all, v_all, bias_ref, query, grad, masks)
            top = top_of(pieces)
            _, total, drift = sums_of(pieces, top)
            row = plan.stat_row(band, group)
            stats_ref[0, row, :] = top
            stats_ref[1, row, :] = total
            stats_ref[2, row, :] = drift


def lon_kernel(
    q_all,
    g_all,
    east_ref,
    west_ref,
    corner_a_ref,
    corner_b_ref,
    bias_ref,
    own_stats_ref,
    to_east_ref,
    to_west_ref,
    stats_ref,
    k_lon,
    score_grad_ref,
    v_lon,
    k_sum,
    v_sum,
    *,
    plan,
):
    deep, tokens, part = plan.deep, plan.tokens, plan.part
    small = jnp.bfloat16
    odd = lax.rem(lax.axis_index("lat"), 2)
    places = [[strip_place(plan.rows, plan.cols, slot_column, side, kv) for kv in range(2)] for side in range(2)]
    for kv, all_ref in ((0, k_lon), (1, v_lon)):
        all_ref[deep : deep + tokens] = (
            dot_nn(places[0][kv], east_ref[...]) + dot_nn(places[1][kv], west_ref[...])
        ).astype(small)

    def corners(north_ref, south_ref):
        for kv, all_ref in ((0, k_lon), (1, v_lon)):
            for corner_ref, at in ((north_ref, 0), (south_ref, deep + tokens)):
                all_ref[at : at + deep] = (
                    dot_nn(places[0][kv][:deep, :part], corner_ref[:part])
                    + dot_nn(places[1][kv][:deep, :part], corner_ref[part:])
                ).astype(small)

    @pl.when(odd == 1)
    def _():
        corners(corner_a_ref, corner_b_ref)

    @pl.when(odd == 0)
    def _():
        corners(corner_b_ref, corner_a_ref)

    masks = edge_masks()
    k_sum[...] = jnp.zeros_like(k_sum)
    v_sum[...] = jnp.zeros_like(v_sum)
    for band in range(plan.bands):
        for group in range(plan.groups):
            lanes = plan.group_lanes(group)
            place = slice(band * plan.band, (band + 1) * plan.band)
            query = plan.stacked(q_all[place, lanes])
            grad = plan.stacked(g_all[place, lanes])
            pieces = score_pieces(plan, band, group, k_lon, v_lon, bias_ref, query, grad, masks)
            row = plan.stat_row(band, group)
            own_top = own_stats_ref[0, row, :]
            top = jnp.maximum(own_top, top_of(pieces))
            weights, total, drift = sums_of(pieces, top)
            shrink = jnp.exp(own_top - top)
            inverse = 1.0 / (total + own_stats_ref[1, row, :] * shrink)
            delta = (drift + own_stats_ref[2, row, :] * shrink) * inverse
            stats_ref[0, row, :] = top
            stats_ref[1, row, :] = inverse
            stats_ref[2, row, :] = delta
            for (start, stop, where, _, slope), weight in zip(pieces, weights):
                if where != 0 and not plan.answers(band):
                    continue
                prob = weight * inverse
                score_grad = (prob * (slope - delta)).astype(small)
                if plan.answers(band):
                    local = slice(start - band * plan.band, stop - band * plan.band)
                    score_grad_ref[band - 1, group, local, :] = score_grad
                if where == 0:
                    mine = slice(start - deep, stop - deep)
                    k_sum[mine, lanes] += dot_nn(score_grad, query)
                    v_sum[mine, lanes] += dot_nn(prob.astype(small), grad)
    k_strip = k_sum[...].astype(small)
    v_strip = v_sum[...].astype(small)
    for side, out_ref in ((0, to_east_ref), (1, to_west_ref)):
        out_ref[...] = (
            dot_nn(strip_pick(plan.rows, plan.cols, slot_column, side, 0), k_strip)
            + dot_nn(strip_pick(plan.rows, plan.cols, slot_column, side, 1), v_strip)
        ).astype(small)


def own_kernel(
    q_all,
    g_all,
    k_all,
    v_all,
    k_lon,
    score_grad_ref,
    bias_ref,
    stats_ref,
    q_grad_ref,
    k_part_ref,
    v_part_ref,
    q_sum,
    *,
    plan,
    scale,
):
    deep, near, tokens = plan.deep, plan.near, plan.tokens
    small = jnp.bfloat16
    masks = edge_masks()
    k_part_ref[...] = jnp.zeros_like(k_part_ref)
    v_part_ref[...] = jnp.zeros_like(v_part_ref)
    for band in range(plan.bands):
        for group in range(plan.groups):
            lanes = plan.group_lanes(group)
            place = slice(band * plan.band, (band + 1) * plan.band)
            query = plan.stacked(q_all[place, lanes])
            grad = plan.stacked(g_all[place, lanes])
            answers = plan.answers(band)
            pieces = score_pieces(
                plan, band, group, k_all, v_all, bias_ref, query, grad, masks, lambda where: answers or where == 0
            )
            row = plan.stat_row(band, group)
            top = stats_ref[0, row, :]
            inverse = stats_ref[1, row, :]
            delta = stats_ref[2, row, :]
            q_part = None
            for start, stop, where, score, slope in pieces:
                prob = jnp.exp(score - top) * inverse
                score_grad = (prob * (slope - delta)).astype(small)
                if where == 0:
                    mine = slice(start - deep, stop - deep)
                    k_part_ref[mine, lanes] += dot_nn(score_grad, query)
                    v_part_ref[mine, lanes] += dot_nn(prob.astype(small), grad)
                if answers:
                    term = dot_tn(score_grad, k_all[start:stop, lanes])
                    q_part = term if q_part is None else q_part + term
            if answers:
                window = slice(band * plan.band, band * plan.band + plan.reach)
                q_part = q_part + dot_tn(score_grad_ref[band - 1, group], k_lon[window, lanes])
                q_sum[place, lanes] = plan.heads_of(q_part)
    q_grad_ref[...] = (q_sum[near : near + tokens] * scale).astype(small)


def finish_kernel(k_part_ref, v_part_ref, from_west_ref, from_east_ref, k_grad_ref, v_grad_ref, *, rows, cols):
    for kv, part_ref, out_ref in ((0, k_part_ref, k_grad_ref), (1, v_part_ref, v_grad_ref)):
        total = part_ref[...]
        total += dot_nn(strip_place(rows, cols, edge_column, 0, kv), from_west_ref[...])
        total += dot_nn(strip_place(rows, cols, edge_column, 1, kv), from_east_ref[...])
        out_ref[...] = total.astype(out_ref.dtype)


def ring(axis, step):
    count = lax.axis_size(axis)
    return [(i, (i + step) % count) for i in range(count)]


def pairs(axis, first):
    count = lax.axis_size(axis)
    partner = list(range(count))
    for i in range(first, count - 1, 2):
        partner[i], partner[i + 1] = i + 1, i
    return [(i, partner[i]) for i in range(count)]


def call(kernel, name, out_shape, in_specs, scratch=(), out_specs=None, limit_mib=24, flops=0, **fixed):
    moved = sum(s.size * s.dtype.itemsize for s in out_shape)
    return pl.pallas_call(
        functools.partial(kernel, **fixed),
        out_shape=out_shape,
        in_specs=in_specs,
        out_specs=out_specs or (VMEM,) * len(out_shape),
        scratch_shapes=list(scratch),
        compiler_params=pltpu.CompilerParams(vmem_limit_bytes=limit_mib * 1024 * 1024),
        cost_estimate=pl.CostEstimate(flops=flops, bytes_accessed=2 * moved, transcendentals=0),
        name=name,
    )


def on_device(queries, keys, values, out_grad, pos_bias):
    rows, cols, width = queries.shape
    heads = pos_bias.shape[0]
    head_size = width // heads
    scale = head_size**-0.5
    plan = Plan(rows, cols, width, head_size)
    small = jnp.bfloat16
    tokens, strip, part = plan.tokens, plan.strip, plan.part
    q, k, v, g = (x.reshape(tokens, width) for x in (queries, keys, values, out_grad))

    def shape(count, dtype=small):
        return jax.ShapeDtypeStruct((count, width), dtype)

    def copies(count):
        return pltpu.SemaphoreType.DMA((count,))

    west_edge, east_edge = call(
        pack_lon_kernel,
        "pack_lon",
        (shape(strip), shape(strip)),
        [ANY, ANY],
        [pltpu.VMEM((tokens, width), small), pltpu.VMEM((tokens, width), small), copies(2)],
        limit_mib=60,
        rows=rows,
        cols=cols,
    )(k, v)
    from_east = lax.ppermute(west_edge, "lon", ring("lon", -1))
    from_west = lax.ppermute(east_edge, "lon", ring("lon", 1))

    lat_size = 2 * plan.deep + 2 * plan.near
    lat_a, lat_b = call(
        pack_lat_kernel,
        "pack_lat",
        (shape(lat_size), shape(lat_size)),
        [ANY] * 5,
        [copies(8)],
        limit_mib=60,
        deep=plan.deep,
        near=plan.near,
    )(k, v, q, g, west_edge)
    halo_a = lax.ppermute(lat_a, "lat", pairs("lat", 0))
    halo_b = lax.ppermute(lat_b, "lat", pairs("lat", 1))

    bias_shape = jax.ShapeDtypeStruct((plan.reach, heads * plan.band), jnp.float32)
    own_bias, lon_bias = call(
        bias_kernel, "bias", (bias_shape, bias_shape), [VMEM, ANY], cols=cols
    )(pos_bias, lat_a)

    corner_a, corner_b = call(
        pack_corner_kernel,
        "pack_corner",
        (shape(2 * part), shape(2 * part)),
        [VMEM, VMEM, ANY],
        flops=6_000_000_000,
        part=part,
    )(from_east, from_west, own_bias)
    corner_halo_a = lax.ppermute(corner_a, "lat", pairs("lat", 0))
    corner_halo_b = lax.ppermute(corner_b, "lat", pairs("lat", 1))

    stats_shape = jax.ShapeDtypeStruct((3, 8 * plan.groups, plan.stack), jnp.float32)
    q_all, g_all, k_all, v_all, own_stats = call(
        own_stats_kernel,
        "own_stats",
        (shape(plan.wide), shape(plan.wide), shape(plan.ext), shape(plan.ext), stats_shape),
        [VMEM] * 7 + [ANY],
        flops=3_000_000_000,
        plan=plan,
        scale=scale,
    )(q, g, k, v, halo_a, halo_b, own_bias, corner_a)

    grads_shape = jax.ShapeDtypeStruct((plan.bands - 2, plan.groups, plan.reach, plan.stack), small)
    to_east, to_west, stats, k_lon, score_grads = call(
        lon_kernel,
        "lon_pairs",
        (shape(strip), shape(strip), stats_shape, shape(plan.ext), grads_shape),
        [VMEM] * 8,
        [
            pltpu.VMEM((plan.ext, width), small),
            pltpu.VMEM((tokens, width), jnp.float32),
            pltpu.VMEM((tokens, width), jnp.float32),
        ],
        flops=4_000_000_000,
        plan=plan,
    )(q_all, g_all, from_east, from_west, corner_halo_a, corner_halo_b, lon_bias, own_stats)
    back_west = lax.ppermute(to_east, "lon", ring("lon", 1))
    back_east = lax.ppermute(to_west, "lon", ring("lon", -1))

    q_grad, k_part, v_part = call(
        own_kernel,
        "own_pairs",
        (shape(tokens), shape(tokens, jnp.float32), shape(tokens, jnp.float32)),
        [VMEM] * 8,
        [pltpu.VMEM((plan.wide, width), jnp.float32)],
        flops=5_000_000_000,
        plan=plan,
        scale=scale,
    )(q_all, g_all, k_all, v_all, k_lon, score_grads, own_bias, stats)

    k_grad, v_grad = call(
        finish_kernel, "finish", (shape(tokens), shape(tokens)), [VMEM] * 4, rows=rows, cols=cols
    )(k_part, v_part, back_west, back_east)
    return tuple(x.reshape(queries.shape) for x in (q_grad, k_grad, v_grad))


def solution(mesh):
    placed = P("lat", "lon", None)
    return jax.shard_map(
        on_device,
        mesh=mesh,
        in_specs=(placed, placed, placed, placed, P()),
        out_specs=(placed, placed, placed),
        check_vma=False,
    )
```
